128 devices in a mesh: pipe: 16 (over x_lo, z, core), tensor: 8 (over x_hi, y).
Axes of the slice: x: 4 (x_hi: 2, x_lo: 2; x = x_hi * 2 + x_lo), y: 4, z: 4, core: 2. Of those that a mesh axis runs over, the one named last changes fastest.
Arguments:
- stashed: bfloat16 [16, 2, 512, 4096], P('pipe', None, 'tensor'), may hold values from -64 to 64
- upstream: bfloat16 [16, 512, 4096], P('pipe', 'tensor'), may hold values from -6 to 6
- loss_grad: bfloat16 [512, 4096], P('tensor'), may hold values from -6 to 6
- norm_gain: float32 [16, 4096], P('pipe'), may hold values from 0.5 to 1.5
- w_query: bfloat16 [16, 4096, 4096], P('pipe', None, 'tensor'), may hold values from -0.09375 to 0.09375
- w_key: bfloat16 [16, 4096, 1024], P('pipe', None, 'tensor'), may hold values from -2.359375 to 2.359375
- w_value: bfloat16 [16, 4096, 1024], P('pipe', None, 'tensor'), may hold values from -0.09375 to 0.09375
- w_out: bfloat16 [16, 4096, 4096], P('pipe', 'tensor'), may hold values from -0.09375 to 0.09375
- evicted_map: int32 [16], replicated, may hold values from 0 to 1, as said below
- plan: int32 [17], replicated, may hold values from 0 to 16, each once
- segments: int32 [17, 512], replicated, may hold values from 0 to 3, never falling along the last dimension, each value on 1 to 256 neighbouring positions
Outputs:
- layer_grads: bfloat16 [16, 2, 512, 4096], P('pipe', None, 'tensor')
The draws below stay inside these ranges and needn't reach their ends.
Inputs may be any that keep to these rules, and one draw needn't show every extreme that they name: `evicted_map`: entry i equals entry 15 - i and entry 0 is 1; where entry i is 1, stashed[i] holds the inputs of section 15 - i.
All inputs are finite; a program needn't handle non-finite values.
Results may differ from the reference program's by a relative error of at most 0.023.
The reference program's roundings to bfloat16 on the way count: a program that leaves them out, or rounds other values in their place, can miss the bound.
Values may be sent and summed in bfloat16 or wider, within the bound.
A program may use at most 128 MiB of HBM per device.

```python
import math
import jax
import jax.numpy as jnp
import numpy as np
from jax import lax

D = 4096
HEADS = 32
KVH = 8
HD = 128
SEQ = 512
MICRO = 17
N_PIPE = 16


def query_base(key):
    return jnp.clip(jax.random.normal(key, (N_PIPE, D, HEADS * HD), jnp.float32), -6.0, 6.0)


def draw_w_query(key, part):
    shared = query_base(key)
    return (shared * D ** (-0.5)).astype(jnp.bfloat16)


def draw_w_key(key, part):
    key = jax.random.fold_in(key, 2)
    own = jnp.clip(jax.random.normal(key, (N_PIPE, D, KVH * HD), jnp.float32), -6.0, 6.0)
    return (own * D ** (-0.5)).astype(jnp.bfloat16)


def draw_stashed(key, part):
    key = jax.random.fold_in(key, 3)
    base = jnp.clip(jax.random.normal(key, (N_PIPE, 2, SEQ, D), jnp.float32), -6.0, 6.0)
    return base.astype(jnp.bfloat16)


def draw_evicted_map(key, part):
    key = jax.random.fold_in(key, 4)
    number = jax.random.randint(key, (), 1, N_PIPE // 2 + 1)
    positions = jnp.arange(N_PIPE)
    return ((positions < number) | (positions >= N_PIPE - number)).astype(jnp.int32)


def steps_of(stream_key, dims, split, low, high):
    loudness, own = 1.0, jax.random.fold_in(stream_key, 6)
    for dim, blocks in split:
        draws = jnp.exp(jax.random.uniform(jax.random.fold_in(own, dim), (blocks,), jnp.float32, low / len(split), high / len(split)))
        loudness = loudness * jnp.repeat(draws, dims[dim] // blocks).reshape([-1 if axis == dim else 1 for axis in range(len(dims))])
    return loudness


def length_profile(count, total, reach, slope):
    weights = [(1 << 20) // math.isqrt(standing ** slope) + 1 for standing in range(2, count + 1)]
    surplus, given = total - reach - (count - 1), [1] * (count - 1)
    while surplus > 0:
        free = [i for i in range(count - 1) if given[i] < reach]
        whole, left = sum([weights[i] for i in free]), surplus
        for i in free:
            extra = min(reach - given[i], max(1, left * weights[i] // whole), surplus)
            given[i] = given[i] + extra
            surplus = surplus - extra
    return np.array([reach] + given)


def uneven(key, amount, total, most, lean):
    if amount == 2:
        one = jax.random.randint(key, (), max(1, total - most), min(most, total - 1) + 1)
        return jnp.stack([one, total - one])
    tallies = jnp.asarray(length_profile(amount, total, most, lean), jnp.int32)
    couples = (amount - 1) // 2
    giver, sink = tallies[1:1 + 2 * couples:2], tallies[2:2 + 2 * couples:2]
    margin = jnp.minimum(giver - 1, most - sink)
    shifted = jax.random.randint(jax.random.fold_in(key, 1), (couples,), 0, 1 << 20) % (margin + 1)
    tallies = tallies.at[1:1 + 2 * couples:2].set(giver - shifted).at[2:2 + 2 * couples:2].set(sink + shifted)
    return tallies[jax.random.permutation(jax.random.fold_in(key, 2), amount)]


def centred(key, shape, deviation, reach, pieces=(), held_as=jnp.bfloat16):
    drawn = deviation * jax.random.normal(key, shape, jnp.float32)
    if pieces:
        drawn = drawn * steps_of(key, shape, pieces, -0.22, 0.18)
    return jnp.clip(drawn, -reach, reach).astype(held_as)


def setup_inputs(seed: int = 0) -> dict:
    keys = jax.random.split(jax.random.key(seed), 12)
    stashed = draw_stashed(jax.random.fold_in(keys[11], 71), 0)
    upstream = centred(keys[1], (N_PIPE, SEQ, D), 1.0, 6.0, ((0, 16), (1, 8)))
    loss_grad = centred(keys[2], (SEQ, D), 1.0, 6.0, ((0, 8),))
    norm_gain = jnp.clip(1.0 + 0.1 * jax.random.normal(keys[3], (N_PIPE, D), jnp.float32), 0.5, 1.5)
    w_query = draw_w_query(jax.random.fold_in(keys[11], 71), 0)
    w_key = draw_w_key(jax.random.fold_in(keys[11], 71), 0)
    w_value = centred(keys[6], (N_PIPE, D, KVH * HD), D ** -0.5, 0.09375, ((0, 16), (2, 8)))
    w_out = centred(keys[7], (N_PIPE, HEADS * HD, D), (HEADS * HD) ** -0.5, 0.09375, ((0, 16), (1, 8)))
    evicted_map = draw_evicted_map(jax.random.fold_in(keys[11], 71), 0)
    plan = jax.random.permutation(keys[9], MICRO).astype(jnp.int32)
    segments = jax.vmap(lambda own: jnp.searchsorted(jnp.cumsum(uneven(own, 4, SEQ, SEQ // 2, 0)), jnp.arange(SEQ), side="right"))(jax.random.split(keys[10], MICRO)).reshape((MICRO, SEQ)).astype(jnp.int32)
    return dict(stashed=stashed, upstream=upstream, loss_grad=loss_grad, norm_gain=norm_gain, w_query=w_query, w_key=w_key, w_value=w_value, w_out=w_out, evicted_map=evicted_map, plan=plan, segments=segments)


EPS = 1e-05

def round_trip(values):
    return lax.optimization_barrier(values.astype(jnp.bfloat16)).astype(jnp.float32)

def norm_parts(inputs):
    widened = inputs.astype(jnp.float32)
    inverse = 1.0 / jnp.sqrt(lax.optimization_barrier(jnp.mean(widened * widened, axis=-1, keepdims=True)) + EPS)
    return (widened * inverse, inverse)

def section_backward(operands):
    inputs, grad_in, gain_row, query_weight, key_weight, value_weight, out_weight, seg_row = operands
    group = HEADS // KVH
    normed, inverse = norm_parts(inputs)
    hidden = (normed * gain_row).astype(jnp.bfloat16)
    query_rows = jnp.dot(hidden, query_weight, preferred_element_type=jnp.float32)
    key_rows = jnp.dot(hidden, key_weight, preferred_element_type=jnp.float32)
    value_rows = jnp.dot(hidden, value_weight, preferred_element_type=jnp.float32)
    query = round_trip(query_rows).reshape(SEQ, KVH, group, HD)
    keys_all = round_trip(key_rows).reshape(SEQ, KVH, HD)
    values_all = round_trip(value_rows).reshape(SEQ, KVH, HD)
    score_scale = 1.0 / math.sqrt(HD)
    scores = jnp.einsum('qkgd,tkd->kgqt', query, keys_all) * score_scale
    positions = jnp.arange(SEQ)
    allowed = (positions[None, :] <= positions[:, None]) & (seg_row[:, None] == seg_row[None, :])
    scores = jnp.where(allowed, scores, -1e+30)
    weights = jnp.exp(scores - lax.optimization_barrier(jnp.max(scores, axis=-1, keepdims=True)))
    weights = weights / lax.optimization_barrier(jnp.sum(weights, axis=-1, keepdims=True))
    rounded = round_trip(weights)
    out_grad = jnp.dot(grad_in, out_weight.T, preferred_element_type=jnp.float32)
    grad_heads = round_trip(out_grad).reshape(SEQ, KVH, group, HD)
    weight_grad = jnp.einsum('qkgd,tkd->kgqt', grad_heads, values_all)
    delta = lax.optimization_barrier(jnp.sum(weights * weight_grad, axis=-1, keepdims=True))
    score_grad = round_trip(weights * (weight_grad - delta) * score_scale)
    query_grad = jnp.einsum('kgqt,tkd->qkgd', score_grad, keys_all).astype(jnp.bfloat16).reshape(SEQ, HEADS * HD)
    key_grad = jnp.einsum('kgqt,qkgd->tkd', score_grad, query).astype(jnp.bfloat16).reshape(SEQ, KVH * HD)
    value_grad = jnp.einsum('kgqt,qkgd->tkd', rounded, grad_heads).astype(jnp.bfloat16).reshape(SEQ, KVH * HD)
    hidden_grad = jnp.dot(query_grad, query_weight.T, preferred_element_type=jnp.float32)
    hidden_grad = hidden_grad + jnp.dot(key_grad, key_weight.T, preferred_element_type=jnp.float32)
    hidden_grad = hidden_grad + jnp.dot(value_grad, value_weight.T, preferred_element_type=jnp.float32)
    scaled = hidden_grad * gain_row
    result = inverse * (scaled - normed * lax.optimization_barrier(jnp.mean(scaled * normed, axis=-1, keepdims=True)))
    return (result + grad_in.astype(jnp.float32)).astype(jnp.bfloat16)

def reference(stashed, upstream, loss_grad, norm_gain, w_query, w_key, w_value, w_out, evicted_map, plan, segments):
    flags = (evicted_map == 1)[:, None, None, None]
    inputs = jnp.where(flags, stashed[::-1], stashed)
    first_seg = segments[plan[:N_PIPE]]
    second_seg = segments[plan[1:]]
    first = lax.map(section_backward, (inputs[:, 0], upstream, norm_gain, w_query, w_key, w_value, w_out, first_seg))
    second_in = jnp.concatenate([first[1:], loss_grad[None]], axis=0)
    second = lax.map(section_backward, (inputs[:, 1], second_in, norm_gain, w_query, w_key, w_value, w_out, second_seg))
    return jnp.stack([first, second], axis=1)
```

```python
import math

import jax
import jax.numpy as jnp
from jax import lax
from jax.experimental import pallas as pl
from jax.experimental.pallas import tpu as pltpu
from jax.sharding import PartitionSpec as P

MESH = pl.DeviceIdType.MESH
HD = 128
EPS = 1e-05
F32 = jnp.float32
BF16 = jnp.bfloat16


class Net:
    def __init__(self, send, recv):
        self.send, self.recv, self.used = send, recv, 0

    def copy(self, src, dst, device):
        i = self.used
        self.used += 1
        return pltpu.make_async_remote_copy(
            src_ref=src,
            dst_ref=dst,
            send_sem=self.send.at[i],
            recv_sem=self.recv.at[i],
            device_id=device,
            device_id_type=MESH,
        )


def kernel(
    stash, upstream, loss, gain, wq, wk, wv, wo, evicted, plan, segs, out,
    w, wout, h0, d0, h1, d1, part, r0, r1, own, mir, lossv, pas, res,
    qs, ogs, kk, vv, dqkv, dk_acc, dv_acc, lsem, ssem, rsem,
):
    p, t = lax.axis_index("pipe"), lax.axis_index("tensor")
    xh, y = t // 4, t % 4
    yp, ym, y2 = (y + 1) % 4, (y + 3) % 4, (y + 2) % 4
    xo = 1 - xh
    to_yp, to_ym, to_x = (p, xh * 4 + yp), (p, xh * 4 + ym), (p, xo * 4 + y)
    to_mirror, to_prev, from_next = (15 - p, t), ((p + 15) % 16, t), ((p + 1) % 16, t)
    net = Net(ssem, rsem)

    def rows(a, b, h):
        return pl.ds(pl.multiple_of((a * 4 + b) * 64 + 32 * h, 32), 32)

    mine = pl.ds(pl.multiple_of(t * 64, 64), 64)

    barrier = pltpu.get_barrier_semaphore()
    for device in (to_yp, to_ym, to_x, to_mirror, from_next):
        pl.semaphore_signal(barrier, inc=1, device_id=device, device_id_type=MESH)

    local = [
        pltpu.make_async_copy(upstream.at[0], d0.at[mine], lsem.at[0]),
        pltpu.make_async_copy(stash.at[0], own, lsem.at[1]),
        pltpu.make_async_copy(wo.at[0], wout, lsem.at[2]),
        pltpu.make_async_copy(wq.at[0], w.at[:, 0:512], lsem.at[3]),
        pltpu.make_async_copy(wk.at[0], w.at[:, 512:640], lsem.at[4]),
        pltpu.make_async_copy(wv.at[0], w.at[:, 640:768], lsem.at[5]),
        pltpu.make_async_copy(loss, lossv, lsem.at[6]),
    ]
    for c in local:
        c.start()
    pl.semaphore_wait(barrier, 5)

    class Gather:
        def __init__(self, g):
            def cp(sl, device):
                return net.copy(g.at[sl], g.at[sl], device)

            self.x = [cp(rows(xh, y, h), to_x) for h in (0, 1)]
            self.a_p = [cp(rows(xh, y, h), to_yp) for h in (0, 1)]
            self.a_m = [cp(rows(xh, y, h), to_ym) for h in (0, 1)]
            self.b_p = [cp(rows(xo, y, h), to_yp) for h in (0, 1)]
            self.b_m = [cp(rows(xo, y, h), to_ym) for h in (0, 1)]
            self.c_p = cp(rows(xh, ym, 0), to_yp)
            self.c_m = cp(rows(xo, yp, 1), to_ym)
            self.e_0 = cp(rows(xh, y2, 0), to_x)
            self.e_1 = cp(rows(xo, y2, 1), to_x)

        def first(self, h):
            self.x[h].start()
            self.a_p[h].start()
            self.a_m[h].start()

        def ev(self, i):
            if i == 0:
                self.first(0)
                self.first(1)
            elif i == 1 or i == 3:
                h = i // 2
                self.x[h].wait_recv()
                self.b_p[h].start()
                self.b_m[h].start()
            elif i == 2:
                self.a_p[0].wait_recv()
                self.c_p.start()
            elif i == 4:
                self.b_m[1].wait_recv()
                self.c_m.start()
            elif i == 5:
                self.c_p.wait_recv()
                self.e_0.start()
            elif i == 6:
                self.c_m.wait_recv()
                self.e_1.start()
            else:
                for c in [self.a_p[1], *self.a_m, *self.b_p, self.b_m[0], self.e_0, self.e_1]:
                    c.wait_recv()

        def drain(self):
            for c in [*self.x, *self.a_p, *self.a_m, *self.b_p, *self.b_m, self.c_p, self.c_m, self.e_0, self.e_1]:
                c.wait_send()

    class Scatter:
        def __init__(self, r):
            def cp(sl, slot, device):
                return net.copy(part.at[sl], r.at[pl.ds(32 * slot, 32)], device)

            self.r = r
            self.c = [
                cp(rows(xo, y2, 0), 0, to_x),
                cp(rows(xh, y2, 1), 1, to_x),
                cp(rows(xh, y2, 0), 2, to_ym),
                cp(rows(xo, y2, 1), 3, to_yp),
                cp(rows(xo, ym, 0), 4, to_ym),
                cp(rows(xo, ym, 1), 5, to_ym),
                cp(rows(xo, yp, 0), 6, to_yp),
                cp(rows(xo, yp, 1), 7, to_yp),
                cp(rows(xh, ym, 0), 8, to_ym),
                cp(rows(xh, ym, 1), 9, to_ym),
                cp(rows(xh, yp, 0), 10, to_yp),
                cp(rows(xh, yp, 1), 11, to_yp),
                cp(rows(xo, y, 0), 12, to_x),
                cp(rows(xo, y, 1), 13, to_x),
            ]

        def start(self, *ids):
            for i in ids:
                self.c[i].start()

        def add(self, sl, *slots):
            for i in slots:
                self.c[i].wait_recv()

            def body(n, carry):
                cols = pl.ds(pl.multiple_of(n * 512, 512), 512)
                total = part[sl, cols].astype(F32)
                for i in slots:
                    total = total + self.r[pl.ds(32 * i, 32), cols].astype(F32)
                part[sl, cols] = total.astype(BF16)
                return carry

            lax.fori_loop(0, 8, body, 0)

        def ev(self, i):
            if i == 1:
                self.add(rows(xh, y2, 0), 0)
                self.start(2)
            elif i == 2:
                self.add(rows(xo, y2, 1), 1)
                self.start(3)
            elif i == 3:
                self.add(rows(xo, y, 0), 4, 6)
                self.start(12)
            elif i == 4:
                self.add(rows(xo, yp, 1), 3)
                self.start(7)
            elif i == 5:
                self.add(rows(xh, ym, 0), 2)
                self.start(8)
            elif i == 6:
                self.add(rows(xo, y, 1), 5, 7)
                self.start(13)

        def drain(self):
            for c in self.c:
                c.wait_send()

    gathers = [Gather(g) for g in (d0, h0, h1, d1)]
    gd0, gh0, gh1, gd1 = gathers
    scatters = [Scatter(r) for r in (r0, r1)]
    mirrors = [
        [net.copy(stash.at[0, m, pl.ds(32 * h, 32)], mir.at[m, pl.ds(32 * h, 32)], to_mirror) for h in (0, 1)]
        for m in (0, 1)
    ]
    passes = [net.copy(res.at[0, pl.ds(32 * h, 32)], pas.at[pl.ds(32 * h, 32)], to_prev) for h in (0, 1)]
    flipped = evicted[p] == 1
    gain_row = gain[...]

    def norm(m, g):
        def body(n, carry):
            sl = pl.ds(pl.multiple_of(n * 16, 16), 16)
            x = jnp.where(flipped, mir[m, sl].astype(F32), own[m, sl].astype(F32))
            own[m, sl] = x.astype(BF16)
            inverse = 1.0 / jnp.sqrt(jnp.mean(x * x, axis=-1, keepdims=True) + EPS)
            g[pl.ds(pl.multiple_of(t * 64 + n * 16, 16), 16)] = (x * inverse * gain_row).astype(BF16)
            return carry

        lax.fori_loop(0, 4, body, 0)

    def norm_back(m, h, g, r):
        def body(n, carry):
            lo = n * 16
            sl = pl.ds(pl.multiple_of(h * 32 + lo, 16), 16)
            row = pl.ds(pl.multiple_of(t * 64 + h * 32 + lo, 16), 16)
            total = part[row].astype(F32)
            for i in (8, 10, 12):
                total = total + r[pl.ds(pl.multiple_of(32 * (i + h) + lo, 16), 16)].astype(F32)
            x = own[m, sl].astype(F32)
            inverse = 1.0 / jnp.sqrt(jnp.mean(x * x, axis=-1, keepdims=True) + EPS)
            normed = x * inverse
            scaled = total * gain_row
            result = inverse * (scaled - normed * jnp.mean(scaled * normed, axis=-1, keepdims=True))
            res[m, sl] = (result + g[row].astype(F32)).astype(BF16)
            return carry

        lax.fori_loop(0, 2, body, 0)

    def project(g):
        def body(n, carry):
            r = jnp.dot(g[pl.ds(pl.multiple_of(n * 256, 256), 256)], w[...], preferred_element_type=F32).astype(BF16)
            sl = pl.ds(pl.multiple_of(n * 256, 256), 256)
            for j in range(4):
                qs[pl.ds(pl.multiple_of(j * 512 + n * 256, 256), 256)] = r[:, j * HD : (j + 1) * HD]
            kk[sl] = r[:, 512:640]
            vv[sl] = r[:, 640:768]
            return carry

        lax.fori_loop(0, 2, body, 0)

    def back_out(g):
        def body(n, carry):
            r = lax.dot_general(
                g[pl.ds(pl.multiple_of(n * 256, 256), 256)], wout[...], (((1,), (1,)), ((), ())),
                preferred_element_type=F32,
            ).astype(BF16)
            for j in range(4):
                ogs[pl.ds(pl.multiple_of(j * 512 + n * 256, 256), 256)] = r[:, j * HD : (j + 1) * HD]
            return carry

        lax.fori_loop(0, 2, body, 0)

    def attend(m):
        seg_row = segs[pl.ds(plan[p + m], 1)]
        seg_col = jnp.broadcast_to(seg_row, (128, 512)).T[:, :1]
        scale = 1.0 / math.sqrt(HD)
        dk_acc[...] = jnp.zeros_like(dk_acc)
        dv_acc[...] = jnp.zeros_like(dv_acc)
        nt = (((1,), (1,)), ((), ()))

        def head(j, carry):
            for b in (0, 1):
                keys = 256 * (b + 1)
                sl = pl.ds(pl.multiple_of(j * 512 + b * 256, 256), 256)
                q, og = qs[sl], ogs[sl]
                k, v = kk[:keys], vv[:keys]
                scores = lax.dot_general(k, q, nt, preferred_element_type=F32) * scale
                kpos = lax.broadcasted_iota(jnp.int32, (keys, 256), 0)
                qpos = lax.broadcasted_iota(jnp.int32, (keys, 256), 1) + b * 256
                allowed = (kpos <= qpos) & (seg_col[:keys] == seg_row[:, b * 256 : (b + 1) * 256])
                scores = jnp.where(allowed, scores, -1e30)
                weights = jnp.exp(scores - jnp.max(scores, axis=0, keepdims=True))
                weights = weights * (1.0 / jnp.sum(weights, axis=0, keepdims=True))
                weight_grad = lax.dot_general(v, og, nt, preferred_element_type=F32)
                delta = jnp.sum(weights * weight_grad, axis=0, keepdims=True)
                score_grad = (weights * (weight_grad - delta) * scale).astype(BF16)
                dv_acc[:keys] += jnp.dot(weights.astype(BF16), og, preferred_element_type=F32)
                dk_acc[:keys] += jnp.dot(score_grad, q, preferred_element_type=F32)
                dq = jnp.dot(k.T, score_grad, preferred_element_type=F32)
                dqkv[j, b * 256 : (b + 1) * 256] = dq.T.astype(BF16)
            return carry

        lax.fori_loop(0, 4, head, 0)
        dqkv[4] = dk_acc[...].astype(BF16)
        dqkv[5] = dv_acc[...].astype(BF16)

    def back_in(b):
        lo, hi = [pl.ds(pl.multiple_of(a * 256 + b * 64, 64), 64) for a in (0, 1)]
        lhs = jnp.concatenate(
            [jnp.concatenate([dqkv[j, sl] for j in range(6)], axis=1) for sl in (lo, hi)], axis=0
        )

        def body(n, carry):
            cols = pl.ds(pl.multiple_of(n * 512, 512), 512)
            r = lax.dot_general(
                lhs, w[cols], (((1,), (1,)), ((), ())), preferred_element_type=F32
            ).astype(BF16)
            part[lo, cols] = r[:64]
            part[hi, cols] = r[64:]
            return carry

        lax.fori_loop(0, 8, body, 0)

    def scatter_first(sc):
        back_in(y2)
        sc.start(0, 1)
        back_in(ym)
        sc.start(4, 5, 9)
        back_in(yp)
        sc.start(6, 10, 11)
        back_in(y)

    for c in mirrors[0]:
        c.start()
    local[0].wait()
    gd0.ev(0)
    gd0.ev(1)
    gd0.ev(2)
    local[1].wait()
    for c in mirrors[0]:
        c.wait_recv()
    norm(0, h0)
    gh0.ev(0)
    for c in mirrors[1]:
        c.start()
    gd0.ev(3)
    gd0.ev(4)
    gh0.ev(1)
    gh0.ev(2)
    gd0.ev(5)
    gd0.ev(6)
    gh0.ev(3)
    gd0.ev(7)
    for c in local[2:]:
        c.wait()
    gh0.ev(4)
    back_out(d0)
    gh0.ev(5)
    for c in mirrors[1]:
        c.wait_recv()
    norm(1, h1)
    gh0.ev(6)
    gh1.ev(0)
    gh0.ev(7)
    project(h0)
    gh1.ev(1)
    gh1.ev(2)
    attend(0)
    gh1.ev(3)
    gh1.ev(4)
    sc = scatters[0]
    scatter_first(sc)
    gh1.ev(5)
    gh1.ev(6)
    sc.ev(1)
    sc.ev(2)
    sc.ev(3)
    sc.ev(4)
    sc.ev(5)
    sc.ev(6)
    gh1.ev(7)
    project(h1)
    for h in (0, 1):
        for i in (8, 10, 12):
            sc.c[i + h].wait_recv()
        norm_back(0, h, d0, r0)
        passes[h].start()
    first_out = pltpu.make_async_copy(res.at[0], out.at[0, 0], lsem.at[7])
    first_out.start()

    last = p == 15
    for h in (0, 1):
        passes[h].wait_recv()
        sl = pl.ds(32 * h, 32)
        d1[rows(xh, y, h)] = jnp.where(last, lossv[sl].astype(F32), pas[sl].astype(F32)).astype(BF16)
        gd1.first(h)
    for i in range(1, 8):
        gd1.ev(i)
    sc.drain()
    back_out(d1)
    attend(1)
    sc = scatters[1]
    scatter_first(sc)
    for i in range(1, 7):
        sc.ev(i)
    for h in (0, 1):
        for i in (8, 10, 12):
            sc.c[i + h].wait_recv()
        norm_back(1, h, d1, r1)
    second_out = pltpu.make_async_copy(res.at[1], out.at[0, 1], lsem.at[8])
    second_out.start()
    sc.drain()
    for g in gathers:
        g.drain()
    for c in [*mirrors[0], *mirrors[1], *passes]:
        c.wait_send()
    first_out.wait()
    second_out.wait()


def on_device(stashed, upstream, loss_grad, norm_gain, w_query, w_key, w_value, w_out, evicted_map, plan, segments):
    hbm = pl.BlockSpec(memory_space=pl.ANY)
    vmem = pl.BlockSpec(memory_space=pltpu.VMEM)
    smem = pl.BlockSpec(memory_space=pltpu.SMEM)
    full = pltpu.VMEM((512, 4096), BF16)
    return pl.pallas_call(
        kernel,
        name="relay_backward",
        out_shape=jax.ShapeDtypeStruct((1, 2, 64, 4096), BF16),
        in_specs=[hbm, hbm, hbm, vmem, hbm, hbm, hbm, hbm, smem, smem, vmem],
        out_specs=hbm,
        scratch_shapes=[
            pltpu.VMEM((4096, 768), BF16),
            full, full, full, full, full, full,
            pltpu.VMEM((448, 4096), BF16),
            pltpu.VMEM((448, 4096), BF16),
            pltpu.VMEM((2, 64, 4096), BF16),
            pltpu.VMEM((2, 64, 4096), BF16),
            pltpu.VMEM((64, 4096), BF16),
            pltpu.VMEM((64, 4096), BF16),
            pltpu.VMEM((2, 64, 4096), BF16),
            pltpu.VMEM((2048, HD), BF16),
            pltpu.VMEM((2048, HD), BF16),
            pltpu.VMEM((512, HD), BF16),
            pltpu.VMEM((512, HD), BF16),
            pltpu.VMEM((6, 512, HD), BF16),
            pltpu.VMEM((512, HD), F32),
            pltpu.VMEM((512, HD), F32),
            pltpu.SemaphoreType.DMA((9,)),
            pltpu.SemaphoreType.DMA((90,)),
            pltpu.SemaphoreType.DMA((90,)),
        ],
        compiler_params=pltpu.CompilerParams(
            collective_id=0, has_side_effects=True, vmem_limit_bytes=60 * 2**20
        ),
        cost_estimate=pl.CostEstimate(flops=20 * 10**9, bytes_accessed=16 * 2**20, transcendentals=2 * 10**6),
    )(stashed, upstream, loss_grad, norm_gain, w_query, w_key, w_value, w_out, evicted_map, plan, segments)


def solution(mesh):
    in_specs = (
        P("pipe", None, "tensor", None),
        P("pipe", "tensor", None),
        P("tensor", None),
        P("pipe", None),
        P("pipe", None, "tensor"),
        P("pipe", None, "tensor"),
        P("pipe", None, "tensor"),
        P("pipe", "tensor", None),
        P(),
        P(),
        P(),
    )
    return jax.shard_map(
        on_device, mesh=mesh, in_specs=in_specs, out_specs=P("pipe", None, "tensor", None), check_vma=False
    )
```

```python
import math

import jax
import jax.numpy as jnp
from jax import lax
from jax.experimental import pallas as pl
from jax.experimental.pallas import tpu as pltpu
from jax.sharding import PartitionSpec as P

MESH = pl.DeviceIdType.MESH
HD = 128
EPS = 1e-05
F32 = jnp.float32
BF16 = jnp.bfloat16


class Net:
    def __init__(self, send, recv):
        self.send, self.recv, self.used = send, recv, 0

    def copy(self, src, dst, device):
        i = self.used
        self.used += 1
        return pltpu.make_async_remote_copy(
            src_ref=src,
            dst_ref=dst,
            send_sem=self.send.at[i],
            recv_sem=self.recv.at[i],
            device_id=device,
            device_id_type=MESH,
        )


def kernel(
    stash, upstream, loss, gain, wq, wk, wv, wo, evicted, plan, segs, out,
    w, wout, h0, d0, h1, d1, part, r0, r1, own, mir, lossv, pas, res,
    qs, ogs, kk, vv, dqkv, dk_acc, dv_acc, bias, probs, lsem, ssem, rsem,
):
    p, t = lax.axis_index("pipe"), lax.axis_index("tensor")
    xh, y = t // 4, t % 4
    yp, ym, y2 = (y + 1) % 4, (y + 3) % 4, (y + 2) % 4
    xo = 1 - xh
    to_yp, to_ym, to_x = (p, xh * 4 + yp), (p, xh * 4 + ym), (p, xo * 4 + y)
    to_mirror, to_prev, from_next = (15 - p, t), ((p + 15) % 16, t), ((p + 1) % 16, t)
    net = Net(ssem, rsem)

    def rows(a, b, h):
        return pl.ds(pl.multiple_of((a * 4 + b) * 64 + 32 * h, 32), 32)

    def part_rows(a, b, h, q):
        return pl.ds(pl.multiple_of((a * 4 + b) * 64 + 32 * h + 16 * q, 16), 16)

    mine = pl.ds(pl.multiple_of(t * 64, 64), 64)

    barrier = pltpu.get_barrier_semaphore()
    for device in (to_yp, to_ym, to_x, to_mirror, from_next):
        pl.semaphore_signal(barrier, inc=1, device_id=device, device_id_type=MESH)

    local = [
        pltpu.make_async_copy(upstream.at[0], d0.at[mine], lsem.at[0]),
        pltpu.make_async_copy(stash.at[0], own, lsem.at[1]),
        pltpu.make_async_copy(wo.at[0], wout, lsem.at[2]),
        pltpu.make_async_copy(wq.at[0], w.at[:, 0:512], lsem.at[3]),
        pltpu.make_async_copy(wk.at[0], w.at[:, 512:640], lsem.at[4]),
        pltpu.make_async_copy(wv.at[0], w.at[:, 640:768], lsem.at[5]),
        pltpu.make_async_copy(loss, lossv, lsem.at[6]),
    ]
    for c in local:
        c.start()
    pl.semaphore_wait(barrier, 5)

    class Gather:
        def __init__(self, g, h, along=False):
            def cp(sl, device):
                return net.copy(g.at[sl], g.at[sl], device)

            self.along = along
            self.x = cp(rows(xh, y, h), to_x)
            self.a_p, self.a_m = cp(rows(xh, y, h), to_yp), cp(rows(xh, y, h), to_ym)
            self.b_p, self.b_m = cp(rows(xo, y, h), to_yp), cp(rows(xo, y, h), to_ym)
            self.c_p, self.c_m = cp(part_rows(xh, ym, h, 0), to_yp), cp(part_rows(xh, yp, h, 1), to_ym)
            if along:
                self.e_p, self.e_m = cp(part_rows(xo, ym, h, 0), to_yp), cp(part_rows(xo, yp, h, 1), to_ym)
                self.ends = (self.e_p, self.e_m)
            else:
                self.e = cp(rows(xh, y2, h), to_x)
                self.ends = (self.e,)

        def near(self):
            self.a_p.start()
            self.a_m.start()

        def far(self):
            self.a_p.wait_recv()
            self.a_m.wait_recv()
            self.c_p.start()
            self.c_m.start()

        def across(self):
            self.x.wait_recv()
            self.b_p.start()
            self.b_m.start()

        def last(self):
            if self.along:
                self.b_p.wait_recv()
                self.e_p.start()
                self.b_m.wait_recv()
                self.e_m.start()
            else:
                self.c_p.wait_recv()
                self.c_m.wait_recv()
                self.e.start()

        def done(self):
            for c in ((self.c_p, self.c_m) if self.along else (self.b_p, self.b_m)) + self.ends:
                c.wait_recv()

        def drain(self):
            for c in (self.x, self.a_p, self.a_m, self.b_p, self.b_m, self.c_p, self.c_m, *self.ends):
                c.wait_send()

    class Scatter:
        def __init__(self, r, h):
            def cp(sl, lo, n, device):
                return net.copy(part.at[sl], r.at[pl.ds(224 * h + lo, n)], device)

            self.r, self.h = r, h
            self.e = cp(rows(xo, y2, h), 0, 32, to_x)
            self.b_m, self.b_p = cp(rows(xo, ym, h), 32, 32, to_ym), cp(rows(xo, yp, h), 64, 32, to_yp)
            self.c_m = cp(part_rows(xh, y2, h, 0), 96, 16, to_ym)
            self.c_p = cp(part_rows(xh, y2, h, 1), 112, 16, to_yp)
            self.a_m, self.a_p = cp(rows(xh, ym, h), 128, 32, to_ym), cp(rows(xh, yp, h), 160, 32, to_yp)
            self.x = cp(rows(xo, y, h), 192, 32, to_x)

        def add(self, sl, n, *los):
            def body(i, carry):
                cols = pl.ds(pl.multiple_of(i * 512, 512), 512)
                total = part[sl, cols].astype(F32)
                for lo in los:
                    total = total + self.r[pl.ds(224 * self.h + lo, n), cols].astype(F32)
                part[sl, cols] = total.astype(BF16)
                return carry

            lax.fori_loop(0, 8, body, 0)

        def far(self):
            self.e.wait_recv()
            self.add(rows(xh, y2, self.h), 32, 0)
            self.c_m.start()
            self.c_p.start()

        def across(self):
            self.b_m.wait_recv()
            self.b_p.wait_recv()
            self.add(rows(xo, y, self.h), 32, 32, 64)
            self.x.start()

        def near(self):
            self.c_m.wait_recv()
            self.add(part_rows(xh, ym, self.h, 0), 16, 96)
            self.a_m.start()
            self.c_p.wait_recv()
            self.add(part_rows(xh, yp, self.h, 1), 16, 112)
            self.a_p.start()

        def done(self):
            for c in (self.a_m, self.a_p, self.x):
                c.wait_recv()

        def drain(self):
            for c in (self.e, self.b_m, self.b_p, self.c_m, self.c_p, self.a_m, self.a_p, self.x):
                c.wait_send()

    gd0 = [Gather(d0, 0), Gather(d0, 1, along=True)]
    gh0, gh1, gd1 = [[Gather(g, h) for h in (0, 1)] for g in (h0, h1, d1)]
    sc0, sc1 = [[Scatter(r, h) for h in (0, 1)] for r in (r0, r1)]
    mirrors = [
        [net.copy(stash.at[0, m, pl.ds(32 * h, 32)], mir.at[m, pl.ds(32 * h, 32)], to_mirror) for h in (0, 1)]
        for m in (0, 1)
    ]
    passes = [net.copy(res.at[0, pl.ds(32 * h, 32)], pas.at[pl.ds(32 * h, 32)], to_prev) for h in (0, 1)]
    flipped = evicted[p] == 1
    gain_row = gain[...]
    nt = (((1,), (1,)), ((), ()))
    scale = 1.0 / math.sqrt(HD)

    def norm(m, h, g):
        def body(n, carry):
            lo = 32 * h + n * 16
            sl = pl.ds(pl.multiple_of(lo, 16), 16)
            x = jnp.where(flipped, mir[m, sl].astype(F32), own[m, sl].astype(F32))
            own[m, sl] = x.astype(BF16)
            inverse = 1.0 / jnp.sqrt(jnp.mean(x * x, axis=-1, keepdims=True) + EPS)
            g[pl.ds(pl.multiple_of(t * 64 + lo, 16), 16)] = (x * inverse * gain_row).astype(BF16)
            return carry

        lax.fori_loop(0, 2, body, 0)

    def norm_back(m, h, g, r):
        def body(n, carry):
            lo = n * 16
            sl = pl.ds(pl.multiple_of(h * 32 + lo, 16), 16)
            row = pl.ds(pl.multiple_of(t * 64 + h * 32 + lo, 16), 16)
            total = part[row].astype(F32)
            for i in (128, 160, 192):
                total = total + r[pl.ds(pl.multiple_of(224 * h + i + lo, 16), 16)].astype(F32)
            x = own[m, sl].astype(F32)
            inverse = 1.0 / jnp.sqrt(jnp.mean(x * x, axis=-1, keepdims=True) + EPS)
            normed = x * inverse
            scaled = total * gain_row
            result = inverse * (scaled - normed * jnp.mean(scaled * normed, axis=-1, keepdims=True))
            res[m, sl] = (result + g[row].astype(F32)).astype(BF16)
            return carry

        lax.fori_loop(0, 2, body, 0)

    def project(g, lo, hi):
        def body(n, carry):
            r = jnp.dot(g[pl.ds(pl.multiple_of(n * 256, 256), 256)], w[...], preferred_element_type=F32).astype(BF16)
            sl = pl.ds(pl.multiple_of(n * 256, 256), 256)
            for j in range(4):
                qs[pl.ds(pl.multiple_of(j * 512 + n * 256, 256), 256)] = r[:, j * HD : (j + 1) * HD]
            kk[sl] = r[:, 512:640]
            vv[sl] = r[:, 640:768]
            return carry

        lax.fori_loop(lo, hi, body, 0)

    def back_out(g):
        def body(n, carry):
            r = lax.dot_general(
                g[pl.ds(pl.multiple_of(n * 256, 256), 256)], wout[...], nt,
                preferred_element_type=F32,
            ).astype(BF16)
            for j in range(4):
                ogs[pl.ds(pl.multiple_of(j * 512 + n * 256, 256), 256)] = r[:, j * HD : (j + 1) * HD]
            return carry

        lax.fori_loop(0, 2, body, 0)

    def mask(m):
        seg_row = segs[pl.ds(plan[p + m], 1)]
        seg_col = jnp.broadcast_to(seg_row, (128, 512)).T[:, :1]
        for b in (0, 1):
            keys = 256 * (b + 1)
            kpos = lax.broadcasted_iota(jnp.int32, (keys, 256), 0)
            qpos = lax.broadcasted_iota(jnp.int32, (keys, 256), 1) + b * 256
            allowed = (kpos <= qpos) & (seg_col[:keys] == seg_row[:, b * 256 : (b + 1) * 256])
            bias[m, 256 * b : 256 * b + keys] = jnp.where(allowed, 0.0, -1e30)

    def forward(m, lo, hi):
        def head(j, carry):
            for b in (0, 1):
                keys = 256 * (b + 1)
                sl = pl.ds(pl.multiple_of(j * 512 + b * 256, 256), 256)
                scores = lax.dot_general(kk[:keys], qs[sl], nt, preferred_element_type=F32) * scale
                scores = scores + bias[m, 256 * b : 256 * b + keys]
                weights = jnp.exp(scores - jnp.max(scores, axis=0, keepdims=True))
                weights = weights * (1.0 / jnp.sum(weights, axis=0, keepdims=True))
                probs[j, 256 * b : 256 * b + keys] = weights
            return carry

        lax.fori_loop(lo, hi, head, 0)

    def backward():
        dk_acc[...] = jnp.zeros_like(dk_acc)
        dv_acc[...] = jnp.zeros_like(dv_acc)

        def head(j, carry):
            for b in (0, 1):
                keys = 256 * (b + 1)
                sl = pl.ds(pl.multiple_of(j * 512 + b * 256, 256), 256)
                q, og = qs[sl], ogs[sl]
                weights = probs[j, 256 * b : 256 * b + keys]
                weight_grad = lax.dot_general(vv[:keys], og, nt, preferred_element_type=F32)
                delta = jnp.sum(weights * weight_grad, axis=0, keepdims=True)
                score_grad = (weights * (weight_grad - delta) * scale).astype(BF16)
                dv_acc[:keys] += jnp.dot(weights.astype(BF16), og, preferred_element_type=F32)
                dk_acc[:keys] += jnp.dot(score_grad, q, preferred_element_type=F32)
                dq = jnp.dot(kk[:keys].T, score_grad, preferred_element_type=F32)
                dqkv[j, b * 256 : (b + 1) * 256] = dq.T.astype(BF16)
            return carry

        lax.fori_loop(0, 4, head, 0)
        dqkv[4] = dk_acc[...].astype(BF16)
        dqkv[5] = dv_acc[...].astype(BF16)

    def back_in(h):
        lhs = jnp.concatenate(
            [
                jnp.concatenate([dqkv[j, 64 * i + 32 * h : 64 * i + 32 * h + 32] for j in range(6)], axis=1)
                for i in range(8)
            ],
            axis=0,
        )

        def body(n, carry):
            cols = pl.ds(pl.multiple_of(n * 512, 512), 512)
            r = lax.dot_general(lhs, w[cols], nt, preferred_element_type=F32).astype(BF16)
            for i in range(8):
                part[64 * i + 32 * h : 64 * i + 32 * h + 32, cols] = r[32 * i : 32 * i + 32]
            return carry

        lax.fori_loop(0, 8, body, 0)

    def passed(h):
        passes[h].wait_recv()
        sl = pl.ds(32 * h, 32)
        d1[rows(xh, y, h)] = jnp.where(last, lossv[sl].astype(F32), pas[sl].astype(F32)).astype(BF16)
        gd1[h].x.start()
        gd1[h].near()

    def scatter_first(sc, h):
        back_in(h)
        for c in (sc[h].b_m, sc[h].b_p, sc[h].e):
            c.start()

    last = p == 15

    for c in mirrors[0]:
        c.start()
    local[0].wait()
    gd0[0].near()
    gd0[1].near()
    mask(0)
    local[1].wait()
    for h in (0, 1):
        mirrors[0][h].wait_recv()
        gd0[h].x.start()
        norm(0, h, h0)
        gd0[h].far()
    gh0[0].near()
    gh0[1].near()
    mask(1)
    for h in (0, 1):
        gd0[h].across()
        gh0[h].x.start()
    gd0[0].last()
    for c in mirrors[1]:
        c.start()
    gh0[0].far()
    gh0[1].far()
    gh0[0].across()
    gh0[1].across()
    gd0[1].last()
    gh0[0].last()
    gh0[1].last()
    for h in (0, 1):
        mirrors[1][h].wait_recv()
        norm(1, h, h1)
        gh1[h].near()
        gh1[h].x.start()
    gd0[0].done()
    gd0[1].done()
    for c in local[2:]:
        c.wait()
    back_out(d0)
    gh0[0].done()
    gh0[1].done()
    project(h0, 0, 2)
    forward(0, 0, 4)
    gh1[0].far()
    gh1[0].across()
    backward()
    scatter_first(sc0, 0)
    gh1[1].far()
    gh1[1].across()
    scatter_first(sc0, 1)
    sc0[0].far()
    sc0[0].across()
    gh1[0].last()
    sc0[0].near()
    sc0[1].far()
    sc0[1].across()
    gh1[1].last()
    sc0[0].done()
    norm_back(0, 0, d0, r0)
    passes[0].start()
    sc0[1].near()
    passed(0)
    gh1[0].done()
    gh1[1].done()
    project(h1, 0, 1)
    sc0[1].done()
    norm_back(0, 1, d0, r0)
    passes[1].start()
    first_out = pltpu.make_async_copy(res.at[0], out.at[0, 0], lsem.at[7])
    first_out.start()
    project(h1, 1, 2)

    gd1[0].far()
    passed(1)
    gd1[0].across()
    forward(1, 0, 2)
    gd1[1].far()
    gd1[0].last()
    gd1[1].across()
    forward(1, 2, 4)
    gd1[1].last()
    for c in sc0:
        c.drain()
    for g in gd1:
        g.done()
    back_out(d1)
    backward()
    scatter_first(sc1, 0)
    scatter_first(sc1, 1)
    sc1[0].far()
    sc1[0].across()
    sc1[1].far()
    sc1[0].near()
    sc1[1].across()
    sc1[1].near()
    for h in (0, 1):
        sc1[h].done()
        norm_back(1, h, d1, r1)
    second_out = pltpu.make_async_copy(res.at[1], out.at[0, 1], lsem.at[8])
    second_out.start()
    for c in [*sc1, *gd0, *gh0, *gh1, *gd1]:
        c.drain()
    for c in [*mirrors[0], *mirrors[1], *passes]:
        c.wait_send()
    first_out.wait()
    second_out.wait()


def on_device(stashed, upstream, loss_grad, norm_gain, w_query, w_key, w_value, w_out, evicted_map, plan, segments):
    hbm = pl.BlockSpec(memory_space=pl.ANY)
    vmem = pl.BlockSpec(memory_space=pltpu.VMEM)
    smem = pl.BlockSpec(memory_space=pltpu.SMEM)
    full = pltpu.VMEM((512, 4096), BF16)
    return pl.pallas_call(
        kernel,
        name="relay_backward",
        out_shape=jax.ShapeDtypeStruct((1, 2, 64, 4096), BF16),
        in_specs=[hbm, hbm, hbm, vmem, hbm, hbm, hbm, hbm, smem, smem, vmem],
        out_specs=hbm,
        scratch_shapes=[
            pltpu.VMEM((4096, 768), BF16),
            full, full, full, full, full, full,
            pltpu.VMEM((448, 4096), BF16),
            pltpu.VMEM((448, 4096), BF16),
            pltpu.VMEM((2, 64, 4096), BF16),
            pltpu.VMEM((2, 64, 4096), BF16),
            pltpu.VMEM((64, 4096), BF16),
            pltpu.VMEM((64, 4096), BF16),
            pltpu.VMEM((2, 64, 4096), BF16),
            pltpu.VMEM((2048, HD), BF16),
            pltpu.VMEM((2048, HD), BF16),
            pltpu.VMEM((512, HD), BF16),
            pltpu.VMEM((512, HD), BF16),
            pltpu.VMEM((6, 512, HD), BF16),
            pltpu.VMEM((512, HD), F32),
            pltpu.VMEM((512, HD), F32),
            pltpu.VMEM((2, 768, 256), F32),
            pltpu.VMEM((4, 768, 256), F32),
            pltpu.SemaphoreType.DMA((9,)),
            pltpu.SemaphoreType.DMA((103,)),
            pltpu.SemaphoreType.DMA((103,)),
        ],
        compiler_params=pltpu.CompilerParams(
            collective_id=0, has_side_effects=True, vmem_limit_bytes=60 * 2**20
        ),
        cost_estimate=pl.CostEstimate(flops=20 * 10**9, bytes_accessed=16 * 2**20, transcendentals=2 * 10**6),
    )(stashed, upstream, loss_grad, norm_gain, w_query, w_key, w_value, w_out, evicted_map, plan, segments)


def solution(mesh):
    in_specs = (
        P("pipe", None, "tensor", None),
        P("pipe", "tensor", None),
        P("tensor", None),
        P("pipe", None),
        P("pipe", None, "tensor"),
        P("pipe", None, "tensor"),
        P("pipe", None, "tensor"),
        P("pipe", "tensor", None),
        P(),
        P(),
        P(),
    )
    return jax.shard_map(
        on_device, mesh=mesh, in_specs=in_specs, out_specs=P("pipe", None, "tensor", None), check_vma=False
    )
```

```python
import math

import jax
import jax.numpy as jnp
from jax import lax
from jax.experimental import pallas as pl
from jax.experimental.pallas import tpu as pltpu
from jax.sharding import PartitionSpec as P

MESH = pl.DeviceIdType.MESH
HD = 128
EPS = 1e-05
F32 = jnp.float32
BF16 = jnp.bfloat16


ORDER = (
    61, 0, 28, 12, 13, 2, 4, 27, 62, 65, 60, 1,
    19, 20, 11, 3, 18, 52, 53, 54, 66, 24, 23, 26,
    22, 58, 31, 57, 7, 55, 56, 30, 64, 5, 32, 10,
    29, 59, 8, 21, 25, 126, 6, 63, 33, 87, 68, 88,
    67, 34, 36, 125, 70, 35, 37, 130, 124, 91, 69, 92,
    71, 129, 38, 39, 40, 41, 72, 75, 74, 9, 73, 42,
    44, 43, 45, 46, 76, 78, 79, 131, 77, 80, 49, 50,
    47, 48, 81, 83, 82, 84, 51, 14, 86, 127, 128, 85,
    16, 15, 96, 95, 89, 93, 17, 134, 94, 101, 90, 132,
    133, 102, 99, 140, 138, 139, 103, 142, 100, 97, 141, 98,
    135, 104, 106, 137, 136, 144, 105, 107, 143, 145, 146, 147,
    148, 149, 108, 111, 150, 113, 110, 109, 152, 153, 154, 155,
    151, 114, 116, 112, 156, 115, 117, 157, 158, 159, 160, 118,
    121, 119, 120, 122, 161, 123,
)
ALONG = ()
MIXED = ("E", "T", )


class Steps:
    def __init__(self, send, recv):
        self.send, self.recv = send, recv
        self.copies, self.needs, self.work = {}, {}, {}
        self.arrived, self.left, self.ran = set(), set(), set()

    def copy(self, name, needs, src, dst, device):
        i = len(self.copies)
        self.needs[name] = tuple(needs)
        self.copies[name] = pltpu.make_async_remote_copy(
            src_ref=src,
            dst_ref=dst,
            send_sem=self.send.at[i],
            recv_sem=self.recv.at[i],
            device_id=device,
            device_id_type=MESH,
        )

    def step(self, name, needs, work):
        self.needs[name] = tuple(needs)
        self.work[name] = work

    def arrive(self, name):
        if name not in self.arrived:
            self.arrived.add(name)
            self.copies[name].wait_recv()

    def leave(self, name):
        if name not in self.left:
            self.left.add(name)
            self.copies[name].wait_send()

    def run(self, order):
        names = list(self.needs)
        assert sorted(order) == list(range(len(names)))
        for i in order:
            name = names[i]
            for need in self.needs[name]:
                assert need in self.ran
                if need in self.copies:
                    self.arrive(need)
            if name in self.copies:
                self.copies[name].start()
            else:
                self.work[name]()
            self.ran.add(name)
        for name in self.copies:
            self.arrive(name)
            self.leave(name)


def kernel(
    stash, upstream, loss, gain, wq, wk, wv, wo, evicted, plan, segs, out,
    w, wout, h0, d0, h1, d1, part, r0, r1, own, mir, lossv, pas, res,
    qs, ogs, kk, vv, dqkv, dk_acc, dv_acc, bias, probs, wt, lsem, ssem, rsem,
):
    p, t = lax.axis_index("pipe"), lax.axis_index("tensor")
    xh, y = t // 4, t % 4
    yp, ym, y2 = (y + 1) % 4, (y + 3) % 4, (y + 2) % 4
    xo = 1 - xh
    to_yp, to_ym, to_x = (p, xh * 4 + yp), (p, xh * 4 + ym), (p, xo * 4 + y)
    to_mirror, to_prev, from_next = (15 - p, t), ((p + 15) % 16, t), ((p + 1) % 16, t)
    steps = Steps(ssem, rsem)

    def rows(a, b, h):
        return pl.ds(pl.multiple_of(h * 256 + (a * 4 + b) * 32, 32), 32)

    def part_rows(a, b, h, q):
        return pl.ds(pl.multiple_of(h * 256 + (a * 4 + b) * 32 + 16 * q, 16), 16)

    def half(h):
        return pl.ds(256 * h, 256)

    barrier = pltpu.get_barrier_semaphore()
    for device in (to_yp, to_ym, to_x, to_mirror, from_next):
        pl.semaphore_signal(barrier, inc=1, device_id=device, device_id_type=MESH)

    local = [
        pltpu.make_async_copy(upstream.at[0, 0:32], d0.at[rows(xh, y, 0)], lsem.at[0]),
        pltpu.make_async_copy(upstream.at[0, 32:64], d0.at[rows(xh, y, 1)], lsem.at[1]),
        pltpu.make_async_copy(stash.at[0], own, lsem.at[2]),
        pltpu.make_async_copy(wo.at[0], wout, lsem.at[3]),
        pltpu.make_async_copy(wq.at[0], w.at[:, 0:512], lsem.at[4]),
        pltpu.make_async_copy(wk.at[0], w.at[:, 512:640], lsem.at[5]),
        pltpu.make_async_copy(wv.at[0], w.at[:, 640:768], lsem.at[6]),
        pltpu.make_async_copy(loss, lossv, lsem.at[7]),
    ]
    for c in local:
        c.start()
    pl.semaphore_wait(barrier, 5)

    def gather(name, g, h, needs, along=False):
        def cp(part, after, sl, device, cols=None):
            at = g.at[sl] if cols is None else g.at[sl, pl.ds(2048 * cols, 2048)]
            steps.copy(name + part, after, at, at, device)

        cp("x", needs, rows(xh, y, h), to_x)
        cp("ap", needs, rows(xh, y, h), to_yp)
        cp("am", needs, rows(xh, y, h), to_ym)
        if name[0] in MIXED and h == 0:
            cp("bp", [name + "x"], part_rows(xo, y, h, 0), to_yp)
            cp("bp2", [name + "x"], part_rows(xo, y, h, 1), to_yp, 0)
            cp("f", [name + "ap"], part_rows(xh, ym, h, 1), to_x, 1)
        else:
            cp("bp", [name + "x"], rows(xo, y, h), to_yp)
        if name[0] in MIXED and h == 1:
            cp("bm", [name + "x"], part_rows(xo, y, h, 1), to_ym)
            cp("bm2", [name + "x"], part_rows(xo, y, h, 0), to_ym, 0)
            cp("f", [name + "am"], part_rows(xh, yp, h, 0), to_x, 1)
        else:
            cp("bm", [name + "x"], rows(xo, y, h), to_ym)
        cp("cp", [name + "ap"], part_rows(xh, ym, h, 0), to_yp)
        cp("cm", [name + "am"], part_rows(xh, yp, h, 1), to_ym)
        if along:
            cp("ep", [name + "bp"], part_rows(xo, ym, h, 0), to_yp)
            cp("em", [name + "bm"], part_rows(xo, yp, h, 1), to_ym)
        else:
            cp("e", [name + "cp", name + "cm"], rows(xh, y2, h), to_x)
        return [n for n in steps.copies if n.startswith(name)]

    def scatter(name, r, h, needs):
        def cp(part_name, after, sl, lo, n, device):
            steps.copy(name + part_name, after, part.at[sl], r.at[pl.ds(224 * h + lo, n)], device)

        def add(step, after, *sums):
            def work():
                for sl, n, first, end, los in sums:

                    def body(i, carry):
                        cols = pl.ds(pl.multiple_of(i * 512, 512), 512)
                        total = part[sl, cols].astype(F32)
                        for lo in los:
                            total = total + r[pl.ds(224 * h + lo, n), cols].astype(F32)
                        part[sl, cols] = total.astype(BF16)
                        return carry

                    lax.fori_loop(first, end, body, 0)

            steps.step(name + step, after, work)

        mixed = name[0] in MIXED

        def first(n, sl, lo, device, rows_of=32, cols=(0, 4096)):
            at = pl.ds(*cols)
            steps.copy(name + n, needs, part.at[sl, at], r.at[pl.ds(224 * h + lo, rows_of), at], device)

        first("e", rows(xo, y2, h), 0, to_x)
        if mixed and h == 0:
            first("bm", part_rows(xo, ym, h, 0), 32, to_ym, 16)
            first("bm2", part_rows(xo, ym, h, 1), 48, to_ym, 16, (0, 2048))
            first("f", part_rows(xo, ym, h, 1), 48, to_x, 16, (2048, 2048))
        else:
            first("bm", rows(xo, ym, h), 32, to_ym)
        if mixed and h == 1:
            first("bp", part_rows(xo, yp, h, 1), 80, to_yp, 16)
            first("bp2", part_rows(xo, yp, h, 0), 64, to_yp, 16, (0, 2048))
            first("f", part_rows(xo, yp, h, 0), 64, to_x, 16, (2048, 2048))
        else:
            first("bp", rows(xo, yp, h), 64, to_yp)
        add("far", [name + "e"], (rows(xh, y2, h), 32, 0, 8, (0,)))
        cp("cm", [name + "far"], part_rows(xh, y2, h, 0), 96, 16, to_ym)
        cp("cp", [name + "far"], part_rows(xh, y2, h, 1), 112, 16, to_yp)
        twos = [name + n for n in ("bm", "bp")]
        if not mixed:
            add("acr", twos, (rows(xo, y, h), 32, 0, 8, (32, 64)))
        elif h == 0:
            add(
                "acr", [*twos, name + "bm2"],
                (part_rows(xo, y, h, 0), 16, 0, 8, (32, 64)),
                (part_rows(xo, y, h, 1), 16, 0, 4, (48, 80)),
                (part_rows(xo, y, h, 1), 16, 4, 8, (80,)),
            )
        else:
            add(
                "acr", [*twos, name + "bp2"],
                (part_rows(xo, y, h, 1), 16, 0, 8, (48, 80)),
                (part_rows(xo, y, h, 0), 16, 0, 4, (32, 64)),
                (part_rows(xo, y, h, 0), 16, 4, 8, (32,)),
            )
        cp("x", [name + "acr"], rows(xo, y, h), 192, 32, to_x)
        via_m, via_p = [], []
        if mixed and h == 0:
            via_m = [(part_rows(xh, ym, h, 1), 16, 4, 8, (48,))]
        if mixed and h == 1:
            via_p = [(part_rows(xh, yp, h, 0), 16, 4, 8, (64,))]
        add("nrm", [name + "cm", *needs] + [name + "f"] * len(via_m), (part_rows(xh, ym, h, 0), 16, 0, 8, (96,)), *via_m)
        cp("am", [name + "nrm"], rows(xh, ym, h), 128, 32, to_ym)
        add("nrp", [name + "cp", *needs] + [name + "f"] * len(via_p), (part_rows(xh, yp, h, 1), 16, 0, 8, (112,)), *via_p)
        cp("ap", [name + "nrp"], rows(xh, yp, h), 160, 32, to_yp)
        return [name + n for n in ("am", "ap", "x", "far", "acr", "nrm", "nrp")]

    flipped = evicted[p] == 1
    gain_row = gain[...]
    nt = (((1,), (1,)), ((), ()))
    scale = 1.0 / math.sqrt(HD)

    def norm(m, h, g):
        def body(n, carry):
            lo = 32 * h + n * 16
            sl = pl.ds(pl.multiple_of(lo, 16), 16)
            x = jnp.where(flipped, mir[m, sl].astype(F32), own[m, sl].astype(F32))
            own[m, sl] = x.astype(BF16)
            inverse = 1.0 / jnp.sqrt(jnp.mean(x * x, axis=-1, keepdims=True) + EPS)
            g[pl.ds(pl.multiple_of(256 * h + t * 32 + n * 16, 16), 16)] = (x * inverse * gain_row).astype(BF16)
            return carry

        lax.fori_loop(0, 2, body, 0)

    def norm_back(m, h, g, r):
        def body(n, carry):
            lo = n * 16
            sl = pl.ds(pl.multiple_of(h * 32 + lo, 16), 16)
            row = pl.ds(pl.multiple_of(256 * h + t * 32 + lo, 16), 16)
            total = part[row].astype(F32)
            for i in (128, 160, 192):
                total = total + r[pl.ds(pl.multiple_of(224 * h + i + lo, 16), 16)].astype(F32)
            x = own[m, sl].astype(F32)
            inverse = 1.0 / jnp.sqrt(jnp.mean(x * x, axis=-1, keepdims=True) + EPS)
            normed = x * inverse
            scaled = total * gain_row
            result = inverse * (scaled - normed * jnp.mean(scaled * normed, axis=-1, keepdims=True))
            res[m, sl] = (result + g[row].astype(F32)).astype(BF16)
            return carry

        lax.fori_loop(0, 2, body, 0)

    def project(g, h):
        r = jnp.dot(g[half(h)], w[...], preferred_element_type=F32).astype(BF16)
        for j in range(4):
            qs[pl.ds(j * 512 + 256 * h, 256)] = r[:, j * HD : (j + 1) * HD]
        kk[half(h)] = r[:, 512:640]
        vv[half(h)] = r[:, 640:768]

    def back_out(g, h):
        r = lax.dot_general(g[half(h)], wout[...], nt, preferred_element_type=F32).astype(BF16)
        for j in range(4):
            ogs[pl.ds(j * 512 + 256 * h, 256)] = r[:, j * HD : (j + 1) * HD]

    def position(r):
        return ((r & 255) >> 5) * 64 + (r >> 8) * 32 + (r & 31)

    def mask(m):
        plain = jnp.broadcast_to(segs[pl.ds(plan[p + m], 1)], (8, 512))
        seg_row = jnp.concatenate([plain[:, 64 * i + 32 * h : 64 * i + 32 * h + 32] for h in (0, 1) for i in range(8)], axis=1)
        seg_col = jnp.broadcast_to(seg_row[:1], (128, 512)).T[:, :1]
        kpos = position(lax.broadcasted_iota(jnp.int32, (512, 256), 0))
        for h in (0, 1):
            qpos = position(lax.broadcasted_iota(jnp.int32, (512, 256), 1) + 256 * h)
            allowed = (kpos <= qpos) & (seg_col == seg_row[:1, 256 * h : 256 * h + 256])
            bias[m, h] = jnp.where(allowed, 0.0, -1e30)

    def forward(m, h):
        def head(j, carry):
            q = qs[pl.ds(pl.multiple_of(j * 512 + h * 256, 256), 256)]
            scores = lax.dot_general(kk[...], q, nt, preferred_element_type=F32) * scale
            scores = scores + bias[m, h]
            weights = jnp.exp(scores - jnp.max(scores, axis=0, keepdims=True))
            probs[j, h] = weights * (1.0 / jnp.sum(weights, axis=0, keepdims=True))
            return carry

        lax.fori_loop(0, 4, head, 0)

    def backward(h):
        if h == 0:
            dk_acc[...] = jnp.zeros_like(dk_acc)
            dv_acc[...] = jnp.zeros_like(dv_acc)

        def head(j, carry):
            sl = pl.ds(pl.multiple_of(j * 512 + h * 256, 256), 256)
            q, og = qs[sl], ogs[sl]
            weights = probs[j, h]
            weight_grad = lax.dot_general(vv[...], og, nt, preferred_element_type=F32)
            delta = jnp.sum(weights * weight_grad, axis=0, keepdims=True)
            score_grad = (weights * (weight_grad - delta) * scale).astype(BF16)
            dv_acc[...] += jnp.dot(weights.astype(BF16), og, preferred_element_type=F32)
            dk_acc[...] += jnp.dot(score_grad, q, preferred_element_type=F32)
            dq = jnp.dot(kk[...].T, score_grad, preferred_element_type=F32)
            dqkv[j, half(h)] = dq.T.astype(BF16)
            return carry

        lax.fori_loop(0, 4, head, 0)
        if h == 1:
            dqkv[4] = dk_acc[...].astype(BF16)
            dqkv[5] = dv_acc[...].astype(BF16)

    def back_in(h):
        lhs = jnp.concatenate([dqkv[j, half(h)] for j in range(6)], axis=1)

        def body(n, carry):
            cols = pl.ds(pl.multiple_of(n * 512, 512), 512)
            part[half(h), cols] = jnp.dot(lhs, wt[:, cols], preferred_element_type=F32).astype(BF16)
            return carry

        lax.fori_loop(0, 8, body, 0)

    def passed(h):
        sl = pl.ds(32 * h, 32)
        d1[rows(xh, y, h)] = jnp.where(last, lossv[sl].astype(F32), pas[sl].astype(F32)).astype(BF16)

    last = p == 15
    waited = set()

    def here(*ids):
        for i in ids:
            if i not in waited:
                waited.add(i)
                local[i].wait()

    outs = [
        [pltpu.make_async_copy(res.at[m, pl.ds(32 * h, 32)], out.at[0, m, pl.ds(32 * h, 32)], lsem.at[8 + 2 * m + h]) for h in (0, 1)]
        for m in (0, 1)
    ]

    def do_norm(m, h):
        here(2)
        norm(m, h, (h0, h1)[m])

    def do_project(m, h):
        here(4, 5, 6)
        project((h0, h1)[m], h)

    def turn(i):
        here(4, 5, 6)

        def body(n, carry):
            sl = pl.ds(pl.multiple_of(1024 * i + 256 * n, 256), 256)
            wt[:, sl] = w[sl].T
            return carry

        lax.fori_loop(0, 4, body, 0)

    def do_back_out(m, h):
        here(3)
        back_out((d0, d1)[m], h)

    def do_back_in(m, h):
        if m:
            for n in [n for n in steps.copies if n.startswith("S%d" % h)]:
                steps.leave(n)
        back_in(h)

    def do_norm_back(m, h):
        norm_back(m, h, (d0, d1)[m], (r0, r1)[m])
        outs[m][h].start()

    def do_passed(h):
        here(7)
        passed(h)

    both = (0, 1)
    for m in both:
        for h in both:
            sl = pl.ds(32 * h, 32)
            steps.copy("M%d%d" % (m, h), [], stash.at[0, m, sl], mir.at[m, sl], to_mirror)
            steps.step("norm%d%d" % (m, h), ["M%d%d" % (m, h)], lambda m=m, h=h: do_norm(m, h))
        steps.step("mask%d" % m, [], lambda m=m: mask(m))
    for i in range(4):
        steps.step("wt%d" % i, [], lambda i=i: turn(i))
    for h in both:
        sl = pl.ds(32 * h, 32)
        steps.copy("P%d" % h, ["nb0%d" % h], res.at[0, sl], pas.at[sl], to_prev)
        steps.step("psd%d" % h, ["P%d" % h], lambda h=h: do_passed(h))
    for m in both:
        prev = ["bwd01"] if m else []
        for h in both:
            ins = gather("HI"[m] + str(h), (h0, h1)[m], h, ["norm%d%d" % (m, h)])
            grads = gather("DE"[m] + str(h), (d0, d1)[m], h, ["psd%d" % h] if m else [], "DE"[m] + str(h) in ALONG)
            steps.step("proj%d%d" % (m, h), ins + prev, lambda m=m, h=h: do_project(m, h))
            steps.step("bout%d%d" % (m, h), grads + prev, lambda m=m, h=h: do_back_out(m, h))
            steps.step(
                "fwd%d%d" % (m, h), ["proj%d0" % m, "proj%d1" % m, "mask%d" % m, *prev], lambda m=m, h=h: forward(m, h)
            )
            steps.step(
                "bwd%d%d" % (m, h),
                ["fwd%d%d" % (m, h), "bout%d%d" % (m, h)] + (["bwd%d0" % m] if h else []) + (["bin00", "bin01"] if m else []),
                lambda h=h: backward(h),
            )
            ready = ["bwd%d0" % m, "bwd%d1" % m, "wt0", "wt1", "wt2", "wt3"] + (["nb00", "nb01"] if m else [])
            steps.step("bin%d%d" % (m, h), ready, lambda m=m, h=h: do_back_in(m, h))
            sums = scatter("ST"[m] + str(h), (r0, r1)[m], h, ["bin%d%d" % (m, h)])
            steps.step("nb%d%d" % (m, h), sums, lambda m=m, h=h: do_norm_back(m, h))

    here(0, 1)
    steps.run(ORDER)
    here(*range(8))
    for m in both:
        for h in both:
            outs[m][h].wait()


def on_device(stashed, upstream, loss_grad, norm_gain, w_query, w_key, w_value, w_out, evicted_map, plan, segments):
    hbm = pl.BlockSpec(memory_space=pl.ANY)
    vmem = pl.BlockSpec(memory_space=pltpu.VMEM)
    smem = pl.BlockSpec(memory_space=pltpu.SMEM)
    full = pltpu.VMEM((512, 4096), BF16)
    return pl.pallas_call(
        kernel,
        name="relay_backward",
        out_shape=jax.ShapeDtypeStruct((1, 2, 64, 4096), BF16),
        in_specs=[hbm, hbm, hbm, vmem, hbm, hbm, hbm, hbm, smem, smem, vmem],
        out_specs=hbm,
        scratch_shapes=[
            pltpu.VMEM((4096, 768), BF16),
            full, full, full, full, full, full,
            pltpu.VMEM((448, 4096), BF16),
            pltpu.VMEM((448, 4096), BF16),
            pltpu.VMEM((2, 64, 4096), BF16),
            pltpu.VMEM((2, 64, 4096), BF16),
            pltpu.VMEM((64, 4096), BF16),
            pltpu.VMEM((64, 4096), BF16),
            pltpu.VMEM((2, 64, 4096), BF16),
            pltpu.VMEM((2048, HD), BF16),
            pltpu.VMEM((2048, HD), BF16),
            pltpu.VMEM((512, HD), BF16),
            pltpu.VMEM((512, HD), BF16),
            pltpu.VMEM((6, 512, HD), BF16),
            pltpu.VMEM((512, HD), F32),
            pltpu.VMEM((512, HD), F32),
            pltpu.VMEM((2, 2, 512, 256), F32),
            pltpu.VMEM((4, 2, 512, 256), F32),
            pltpu.VMEM((768, 4096), BF16),
            pltpu.SemaphoreType.DMA((12,)),
            pltpu.SemaphoreType.DMA((110,)),
            pltpu.SemaphoreType.DMA((110,)),
        ],
        compiler_params=pltpu.CompilerParams(
            collective_id=0, has_side_effects=True, vmem_limit_bytes=60 * 2**20
        ),
        cost_estimate=pl.CostEstimate(flops=20 * 10**9, bytes_accessed=16 * 2**20, transcendentals=2 * 10**6),
    )(stashed, upstream, loss_grad, norm_gain, w_query, w_key, w_value, w_out, evicted_map, plan, segments)


def solution(mesh):
    in_specs = (
        P("pipe", None, "tensor", None),
        P("pipe", "tensor", None),
        P("tensor", None),
        P("pipe", None),
        P("pipe", None, "tensor"),
        P("pipe", None, "tensor"),
        P("pipe", None, "tensor"),
        P("pipe", "tensor", None),
        P(),
        P(),
        P(),
    )
    return jax.shard_map(
        on_device, mesh=mesh, in_specs=in_specs, out_specs=P("pipe", None, "tensor", None), check_vma=False
    )
```

```python
import math

import jax
import jax.numpy as jnp
from jax import lax
from jax.experimental import pallas as pl
from jax.experimental.pallas import tpu as pltpu
from jax.sharding import PartitionSpec as P

MESH = pl.DeviceIdType.MESH
HD = 128
EPS = 1e-05
F32 = jnp.float32
BF16 = jnp.bfloat16


ORDER = (
    27, 0, 28, 11, 62, 12, 13, 61, 2, 1, 20, 19,
    26, 9, 3, 52, 31, 66, 54, 53, 18, 23, 60, 30,
    7, 29, 55, 57, 24, 5, 22, 58, 10, 25, 56, 63,
    8, 59, 4, 21, 64, 65, 32, 6, 33, 88, 34, 125,
    126, 67, 68, 36, 35, 37, 87, 129, 70, 92, 124, 69,
    130, 71, 38, 39, 41, 40, 91, 72, 74, 75, 73, 42,
    44, 43, 45, 76, 77, 46, 78, 47, 49, 50, 48, 81,
    131, 83, 82, 79, 80, 84, 51, 128, 127, 14, 93, 15,
    86, 85, 16, 95, 96, 17, 94, 134, 133, 102, 90, 101,
    132, 99, 89, 138, 103, 140, 139, 142, 100, 97, 104, 135,
    98, 141, 106, 136, 144, 137, 105, 107, 143, 145, 146, 147,
    148, 149, 150, 108, 110, 109, 113, 111, 152, 153, 154, 151,
    114, 155, 115, 116, 156, 112, 117, 159, 160, 157, 158, 121,
    118, 122, 119, 120, 161, 123,
)
ALONG = ()
MIXED = ("E", "T", )


class Steps:
    def __init__(self, send, recv):
        self.send, self.recv = send, recv
        self.copies, self.needs, self.work = {}, {}, {}
        self.arrived, self.left, self.ran = set(), set(), set()

    def copy(self, name, needs, src, dst, device):
        i = len(self.copies)
        self.needs[name] = tuple(needs)
        self.copies[name] = pltpu.make_async_remote_copy(
            src_ref=src,
            dst_ref=dst,
            send_sem=self.send.at[i],
            recv_sem=self.recv.at[i],
            device_id=device,
            device_id_type=MESH,
        )

    def step(self, name, needs, work):
        self.needs[name] = tuple(needs)
        self.work[name] = work

    def arrive(self, name):
        if name not in self.arrived:
            self.arrived.add(name)
            self.copies[name].wait_recv()

    def leave(self, name):
        if name not in self.left:
            self.left.add(name)
            self.copies[name].wait_send()

    def run(self, order):
        names = list(self.needs)
        assert sorted(order) == list(range(len(names)))
        for i in order:
            name = names[i]
            for need in self.needs[name]:
                assert need in self.ran
                if need in self.copies:
                    self.arrive(need)
            if name in self.copies:
                self.copies[name].start()
            else:
                self.work[name]()
            self.ran.add(name)
        for name in self.copies:
            self.arrive(name)
            self.leave(name)


def kernel(
    stash, upstream, loss, gain, wq, wk, wv, wo, evicted, plan, segs, out,
    w, wout, h0, d0, h1, d1, part, r0, r1, own, mir, lossv, pas, res,
    qs, ogs, kk, vv, dqkv, dk_acc, dv_acc, bias, probs, wt, lsem, ssem, rsem,
):
    p, t = lax.axis_index("pipe"), lax.axis_index("tensor")
    xh, y = t // 4, t % 4
    yp, ym, y2 = (y + 1) % 4, (y + 3) % 4, (y + 2) % 4
    xo = 1 - xh
    to_yp, to_ym, to_x = (p, xh * 4 + yp), (p, xh * 4 + ym), (p, xo * 4 + y)
    to_mirror, to_prev, from_next = (15 - p, t), ((p + 15) % 16, t), ((p + 1) % 16, t)
    steps = Steps(ssem, rsem)

    def rows(a, b, h):
        return pl.ds(pl.multiple_of(h * 256 + (a * 4 + b) * 32, 32), 32)

    def part_rows(a, b, h, q):
        return pl.ds(pl.multiple_of(h * 256 + (a * 4 + b) * 32 + 16 * q, 16), 16)

    def half(h):
        return pl.ds(256 * h, 256)

    barrier = pltpu.get_barrier_semaphore()
    for device in (to_yp, to_ym, to_x, to_mirror, from_next):
        pl.semaphore_signal(barrier, inc=1, device_id=device, device_id_type=MESH)

    local = [
        pltpu.make_async_copy(upstream.at[0, 0:32], d0.at[rows(xh, y, 0)], lsem.at[0]),
        pltpu.make_async_copy(upstream.at[0, 32:64], d0.at[rows(xh, y, 1)], lsem.at[1]),
        pltpu.make_async_copy(stash.at[0], own, lsem.at[2]),
        pltpu.make_async_copy(wo.at[0], wout, lsem.at[3]),
        pltpu.make_async_copy(wq.at[0], w.at[:, 0:512], lsem.at[4]),
        pltpu.make_async_copy(wk.at[0], w.at[:, 512:640], lsem.at[5]),
        pltpu.make_async_copy(wv.at[0], w.at[:, 640:768], lsem.at[6]),
        pltpu.make_async_copy(loss, lossv, lsem.at[7]),
    ]
    for c in local:
        c.start()
    pl.semaphore_wait(barrier, 5)

    def gather(name, g, h, needs, along=False):
        def cp(part, after, sl, device, cols=None):
            at = g.at[sl] if cols is None else g.at[sl, pl.ds(2048 * cols, 2048)]
            steps.copy(name + part, after, at, at, device)

        cp("x", needs, rows(xh, y, h), to_x)
        cp("ap", needs, rows(xh, y, h), to_yp)
        cp("am", needs, rows(xh, y, h), to_ym)
        if name[0] in MIXED and h == 0:
            cp("bp", [name + "x"], part_rows(xo, y, h, 0), to_yp)
            cp("bp2", [name + "x"], part_rows(xo, y, h, 1), to_yp, 0)
            cp("f", [name + "ap"], part_rows(xh, ym, h, 1), to_x, 1)
        else:
            cp("bp", [name + "x"], rows(xo, y, h), to_yp)
        if name[0] in MIXED and h == 1:
            cp("bm", [name + "x"], part_rows(xo, y, h, 1), to_ym)
            cp("bm2", [name + "x"], part_rows(xo, y, h, 0), to_ym, 0)
            cp("f", [name + "am"], part_rows(xh, yp, h, 0), to_x, 1)
        else:
            cp("bm", [name + "x"], rows(xo, y, h), to_ym)
        cp("cp", [name + "ap"], part_rows(xh, ym, h, 0), to_yp)
        cp("cm", [name + "am"], part_rows(xh, yp, h, 1), to_ym)
        if along:
            cp("ep", [name + "bp"], part_rows(xo, ym, h, 0), to_yp)
            cp("em", [name + "bm"], part_rows(xo, yp, h, 1), to_ym)
        else:
            cp("e", [name + "cp", name + "cm"], rows(xh, y2, h), to_x)
        return [n for n in steps.copies if n.startswith(name)]

    def scatter(name, r, h, needs):
        def cp(part_name, after, sl, lo, n, device):
            steps.copy(name + part_name, after, part.at[sl], r.at[pl.ds(224 * h + lo, n)], device)

        def add(step, after, *sums):
            def work():
                for sl, n, first, end, los in sums:

                    def body(i, carry):
                        cols = pl.ds(pl.multiple_of(i * 512, 512), 512)
                        total = part[sl, cols].astype(F32)
                        for lo in los:
                            total = total + r[pl.ds(224 * h + lo, n), cols].astype(F32)
                        part[sl, cols] = total.astype(BF16)
                        return carry

                    lax.fori_loop(first, end, body, 0)

            steps.step(name + step, after, work)

        mixed = name[0] in MIXED

        def first(n, sl, lo, device, rows_of=32, cols=(0, 4096)):
            at = pl.ds(*cols)
            steps.copy(name + n, needs, part.at[sl, at], r.at[pl.ds(224 * h + lo, rows_of), at], device)

        first("e", rows(xo, y2, h), 0, to_x)
        if mixed and h == 0:
            first("bm", part_rows(xo, ym, h, 0), 32, to_ym, 16)
            first("bm2", part_rows(xo, ym, h, 1), 48, to_ym, 16, (0, 2048))
            first("f", part_rows(xo, ym, h, 1), 48, to_x, 16, (2048, 2048))
        else:
            first("bm", rows(xo, ym, h), 32, to_ym)
        if mixed and h == 1:
            first("bp", part_rows(xo, yp, h, 1), 80, to_yp, 16)
            first("bp2", part_rows(xo, yp, h, 0), 64, to_yp, 16, (0, 2048))
            first("f", part_rows(xo, yp, h, 0), 64, to_x, 16, (2048, 2048))
        else:
            first("bp", rows(xo, yp, h), 64, to_yp)
        add("far", [name + "e"], (rows(xh, y2, h), 32, 0, 8, (0,)))
        cp("cm", [name + "far"], part_rows(xh, y2, h, 0), 96, 16, to_ym)
        cp("cp", [name + "far"], part_rows(xh, y2, h, 1), 112, 16, to_yp)
        twos = [name + n for n in ("bm", "bp")]
        if not mixed:
            add("acr", twos, (rows(xo, y, h), 32, 0, 8, (32, 64)))
        elif h == 0:
            add(
                "acr", [*twos, name + "bm2"],
                (part_rows(xo, y, h, 0), 16, 0, 8, (32, 64)),
                (part_rows(xo, y, h, 1), 16, 0, 4, (48, 80)),
                (part_rows(xo, y, h, 1), 16, 4, 8, (80,)),
            )
        else:
            add(
                "acr", [*twos, name + "bp2"],
                (part_rows(xo, y, h, 1), 16, 0, 8, (48, 80)),
                (part_rows(xo, y, h, 0), 16, 0, 4, (32, 64)),
                (part_rows(xo, y, h, 0), 16, 4, 8, (32,)),
            )
        cp("x", [name + "acr"], rows(xo, y, h), 192, 32, to_x)
        via_m, via_p = [], []
        if mixed and h == 0:
            via_m = [(part_rows(xh, ym, h, 1), 16, 4, 8, (48,))]
        if mixed and h == 1:
            via_p = [(part_rows(xh, yp, h, 0), 16, 4, 8, (64,))]
        add("nrm", [name + "cm", *needs] + [name + "f"] * len(via_m), (part_rows(xh, ym, h, 0), 16, 0, 8, (96,)), *via_m)
        cp("am", [name + "nrm"], rows(xh, ym, h), 128, 32, to_ym)
        add("nrp", [name + "cp", *needs] + [name + "f"] * len(via_p), (part_rows(xh, yp, h, 1), 16, 0, 8, (112,)), *via_p)
        cp("ap", [name + "nrp"], rows(xh, yp, h), 160, 32, to_yp)
        return [name + n for n in ("am", "ap", "x", "far", "acr", "nrm", "nrp")]

    flipped = evicted[p] == 1
    gain_row = gain[...]
    nt = (((1,), (1,)), ((), ()))
    scale = 1.0 / math.sqrt(HD)

    def norm(m, h, g):
        def body(n, carry):
            lo = 32 * h + n * 16
            sl = pl.ds(pl.multiple_of(lo, 16), 16)
            x = jnp.where(flipped, mir[m, sl].astype(F32), own[m, sl].astype(F32))
            own[m, sl] = x.astype(BF16)
            inverse = 1.0 / jnp.sqrt(jnp.mean(x * x, axis=-1, keepdims=True) + EPS)
            g[pl.ds(pl.multiple_of(256 * h + t * 32 + n * 16, 16), 16)] = (x * inverse * gain_row).astype(BF16)
            return carry

        lax.fori_loop(0, 2, body, 0)

    def norm_back(m, h, g, r):
        def body(n, carry):
            lo = n * 16
            sl = pl.ds(pl.multiple_of(h * 32 + lo, 16), 16)
            row = pl.ds(pl.multiple_of(256 * h + t * 32 + lo, 16), 16)
            total = part[row].astype(F32)
            for i in (128, 160, 192):
                total = total + r[pl.ds(pl.multiple_of(224 * h + i + lo, 16), 16)].astype(F32)
            x = own[m, sl].astype(F32)
            inverse = 1.0 / jnp.sqrt(jnp.mean(x * x, axis=-1, keepdims=True) + EPS)
            normed = x * inverse
            scaled = total * gain_row
            result = inverse * (scaled - normed * jnp.mean(scaled * normed, axis=-1, keepdims=True))
            res[m, sl] = (result + g[row].astype(F32)).astype(BF16)
            return carry

        lax.fori_loop(0, 2, body, 0)

    def project(g, h):
        r = jnp.dot(g[half(h)], w[...], preferred_element_type=F32).astype(BF16)
        for j in range(4):
            qs[pl.ds(j * 512 + 256 * h, 256)] = r[:, j * HD : (j + 1) * HD]
        kk[half(h)] = r[:, 512:640]
        vv[half(h)] = r[:, 640:768]

    def back_out(g, h):
        r = lax.dot_general(g[half(h)], wout[...], nt, preferred_element_type=F32).astype(BF16)
        for j in range(4):
            ogs[pl.ds(j * 512 + 256 * h, 256)] = r[:, j * HD : (j + 1) * HD]

    def position(r):
        return ((r & 255) >> 5) * 64 + (r >> 8) * 32 + (r & 31)

    def mask(m):
        plain = jnp.broadcast_to(segs[pl.ds(plan[p + m], 1)], (8, 512))
        seg_row = jnp.concatenate([plain[:, 64 * i + 32 * h : 64 * i + 32 * h + 32] for h in (0, 1) for i in range(8)], axis=1)
        seg_col = jnp.broadcast_to(seg_row[:1], (128, 512)).T[:, :1]
        kpos = position(lax.broadcasted_iota(jnp.int32, (512, 256), 0))
        for h in (0, 1):
            qpos = position(lax.broadcasted_iota(jnp.int32, (512, 256), 1) + 256 * h)
            allowed = (kpos <= qpos) & (seg_col == seg_row[:1, 256 * h : 256 * h + 256])
            bias[m, h] = jnp.where(allowed, 0.0, -1e30)

    def forward(m, h):
        def head(j, carry):
            q = qs[pl.ds(pl.multiple_of(j * 512 + h * 256, 256), 256)]
            scores = lax.dot_general(kk[...], q, nt, preferred_element_type=F32) * scale
            scores = scores + bias[m, h]
            weights = jnp.exp(scores - jnp.max(scores, axis=0, keepdims=True))
            probs[j, h] = weights * (1.0 / jnp.sum(weights, axis=0, keepdims=True))
            return carry

        lax.fori_loop(0, 4, head, 0)

    def backward(h):
        if h == 0:
            dk_acc[...] = jnp.zeros_like(dk_acc)
            dv_acc[...] = jnp.zeros_like(dv_acc)

        def head(j, carry):
            sl = pl.ds(pl.multiple_of(j * 512 + h * 256, 256), 256)
            q, og = qs[sl], ogs[sl]
            weights = probs[j, h]
            weight_grad = lax.dot_general(vv[...], og, nt, preferred_element_type=F32)
            delta = jnp.sum(weights * weight_grad, axis=0, keepdims=True)
            score_grad = (weights * (weight_grad - delta) * scale).astype(BF16)
            dv_acc[...] += jnp.dot(weights.astype(BF16), og, preferred_element_type=F32)
            dk_acc[...] += jnp.dot(score_grad, q, preferred_element_type=F32)
            dq = jnp.dot(kk[...].T, score_grad, preferred_element_type=F32)
            dqkv[j, half(h)] = dq.T.astype(BF16)
            return carry

        lax.fori_loop(0, 4, head, 0)
        if h == 1:
            dqkv[4] = dk_acc[...].astype(BF16)
            dqkv[5] = dv_acc[...].astype(BF16)

    def back_in(h):
        lhs = jnp.concatenate([dqkv[j, half(h)] for j in range(6)], axis=1)

        def body(n, carry):
            cols = pl.ds(pl.multiple_of(n * 512, 512), 512)
            part[half(h), cols] = jnp.dot(lhs, wt[:, cols], preferred_element_type=F32).astype(BF16)
            return carry

        lax.fori_loop(0, 8, body, 0)

    def passed(h):
        sl = pl.ds(32 * h, 32)
        d1[rows(xh, y, h)] = jnp.where(last, lossv[sl].astype(F32), pas[sl].astype(F32)).astype(BF16)

    last = p == 15
    waited = set()

    def here(*ids):
        for i in ids:
            if i not in waited:
                waited.add(i)
                local[i].wait()

    outs = [
        [pltpu.make_async_copy(res.at[m, pl.ds(32 * h, 32)], out.at[0, m, pl.ds(32 * h, 32)], lsem.at[8 + 2 * m + h]) for h in (0, 1)]
        for m in (0, 1)
    ]

    def do_norm(m, h):
        here(2)
        norm(m, h, (h0, h1)[m])

    def do_project(m, h):
        here(4, 5, 6)
        project((h0, h1)[m], h)

    def turn(i):
        here(4, 5, 6)

        def body(n, carry):
            sl = pl.ds(pl.multiple_of(1024 * i + 256 * n, 256), 256)
            wt[:, sl] = w[sl].T
            return carry

        lax.fori_loop(0, 4, body, 0)

    def do_back_out(m, h):
        here(3)
        back_out((d0, d1)[m], h)

    def do_back_in(m, h):
        if m:
            for n in [n for n in steps.copies if n.startswith("S%d" % h)]:
                steps.leave(n)
        back_in(h)

    def do_norm_back(m, h):
        norm_back(m, h, (d0, d1)[m], (r0, r1)[m])
        outs[m][h].start()

    def do_passed(h):
        here(7)
        passed(h)

    both = (0, 1)
    for m in both:
        for h in both:
            sl = pl.ds(32 * h, 32)
            steps.copy("M%d%d" % (m, h), [], stash.at[0, m, sl], mir.at[m, sl], to_mirror)
            steps.step("norm%d%d" % (m, h), ["M%d%d" % (m, h)], lambda m=m, h=h: do_norm(m, h))
        steps.step("mask%d" % m, [], lambda m=m: mask(m))
    for i in range(4):
        steps.step("wt%d" % i, [], lambda i=i: turn(i))
    for h in both:
        sl = pl.ds(32 * h, 32)
        steps.copy("P%d" % h, ["nb0%d" % h], res.at[0, sl], pas.at[sl], to_prev)
        steps.step("psd%d" % h, ["P%d" % h], lambda h=h: do_passed(h))
    for m in both:
        prev = ["bwd01"] if m else []
        for h in both:
            ins = gather("HI"[m] + str(h), (h0, h1)[m], h, ["norm%d%d" % (m, h)])
            grads = gather("DE"[m] + str(h), (d0, d1)[m], h, ["psd%d" % h] if m else [], "DE"[m] + str(h) in ALONG)
            steps.step("proj%d%d" % (m, h), ins + prev, lambda m=m, h=h: do_project(m, h))
            steps.step("bout%d%d" % (m, h), grads + prev, lambda m=m, h=h: do_back_out(m, h))
            steps.step(
                "fwd%d%d" % (m, h), ["proj%d0" % m, "proj%d1" % m, "mask%d" % m, *prev], lambda m=m, h=h: forward(m, h)
            )
            steps.step(
                "bwd%d%d" % (m, h),
                ["fwd%d%d" % (m, h), "bout%d%d" % (m, h)] + (["bwd%d0" % m] if h else []) + (["bin00", "bin01"] if m else []),
                lambda h=h: backward(h),
            )
            ready = ["bwd%d0" % m, "bwd%d1" % m, "wt0", "wt1", "wt2", "wt3"] + (["nb00", "nb01"] if m else [])
            steps.step("bin%d%d" % (m, h), ready, lambda m=m, h=h: do_back_in(m, h))
            sums = scatter("ST"[m] + str(h), (r0, r1)[m], h, ["bin%d%d" % (m, h)])
            steps.step("nb%d%d" % (m, h), sums, lambda m=m, h=h: do_norm_back(m, h))

    here(0, 1)
    steps.run(ORDER)
    here(*range(8))
    for m in both:
        for h in both:
            outs[m][h].wait()


def on_device(stashed, upstream, loss_grad, norm_gain, w_query, w_key, w_value, w_out, evicted_map, plan, segments):
    hbm = pl.BlockSpec(memory_space=pl.ANY)
    vmem = pl.BlockSpec(memory_space=pltpu.VMEM)
    smem = pl.BlockSpec(memory_space=pltpu.SMEM)
    full = pltpu.VMEM((512, 4096), BF16)
    return pl.pallas_call(
        kernel,
        name="relay_backward",
        out_shape=jax.ShapeDtypeStruct((1, 2, 64, 4096), BF16),
        in_specs=[hbm, hbm, hbm, vmem, hbm, hbm, hbm, hbm, smem, smem, vmem],
        out_specs=hbm,
        scratch_shapes=[
            pltpu.VMEM((4096, 768), BF16),
            full, full, full, full, full, full,
            pltpu.VMEM((448, 4096), BF16),
            pltpu.VMEM((448, 4096), BF16),
            pltpu.VMEM((2, 64, 4096), BF16),
            pltpu.VMEM((2, 64, 4096), BF16),
            pltpu.VMEM((64, 4096), BF16),
            pltpu.VMEM((64, 4096), BF16),
            pltpu.VMEM((2, 64, 4096), BF16),
            pltpu.VMEM((2048, HD), BF16),
            pltpu.VMEM((2048, HD), BF16),
            pltpu.VMEM((512, HD), BF16),
            pltpu.VMEM((512, HD), BF16),
            pltpu.VMEM((6, 512, HD), BF16),
            pltpu.VMEM((512, HD), F32),
            pltpu.VMEM((512, HD), F32),
            pltpu.VMEM((2, 2, 512, 256), F32),
            pltpu.VMEM((4, 2, 512, 256), F32),
            pltpu.VMEM((768, 4096), BF16),
            pltpu.SemaphoreType.DMA((12,)),
            pltpu.SemaphoreType.DMA((110,)),
            pltpu.SemaphoreType.DMA((110,)),
        ],
        compiler_params=pltpu.CompilerParams(
            collective_id=0, has_side_effects=True, vmem_limit_bytes=60 * 2**20
        ),
        cost_estimate=pl.CostEstimate(flops=20 * 10**9, bytes_accessed=16 * 2**20, transcendentals=2 * 10**6),
    )(stashed, upstream, loss_grad, norm_gain, w_query, w_key, w_value, w_out, evicted_map, plan, segments)


def solution(mesh):
    in_specs = (
        P("pipe", None, "tensor", None),
        P("pipe", "tensor", None),
        P("tensor", None),
        P("pipe", None),
        P("pipe", None, "tensor"),
        P("pipe", None, "tensor"),
        P("pipe", None, "tensor"),
        P("pipe", "tensor", None),
        P(),
        P(),
        P(),
    )
    return jax.shard_map(
        on_device, mesh=mesh, in_specs=in_specs, out_specs=P("pipe", None, "tensor", None), check_vma=False
    )
```
